32 devices in a mesh: dp: 8 (over y, x, core), seq: 4 (over z).
Axes of the slice: x: 2, y: 2, z: 4, core: 2. Of those that a mesh axis runs over, the one named last changes fastest.
Arguments:
- tokens: bfloat16 [8, 1024, 1280], P('dp', 'seq'), may hold values from -6 to 6
- cotangent: bfloat16 [8, 1024, 1280], P('dp', 'seq'), may hold values from -6 to 6
- weight_inproj: float32 [1, 1280, 3840], P(None, 'dp', 'seq'), may hold values from -0.15625 to 0.15625
- first_inproj: float32 [1, 1280, 3840], P(None, 'dp', 'seq'), may hold values from -8 to 8
- second_inproj: float32 [1, 1280, 3840], P(None, 'dp', 'seq'), may hold values from 9.68 to 38.48
- weight_outproj: float32 [1, 1280, 1280], P(None, 'dp', 'seq'), may hold values from -0.625 to 0.625
- first_outproj: float32 [1, 1280, 1280], P(None, 'dp', 'seq'), may hold values from -16 to 16
- second_outproj: float32 [1, 1280, 1280], P(None, 'dp', 'seq'), may hold values from 38.5024 to 155.648
- weight_expand: float32 [1, 1280, 5120], P(None, 'dp', 'seq'), may hold values from -0.15625 to 0.15625
- first_expand: float32 [1, 1280, 5120], P(None, 'dp', 'seq'), may hold values from -16 to 16
- second_expand: float32 [1, 1280, 5120], P(None, 'dp', 'seq'), may hold values from 38.5024 to 155.648
- weight_contract: float32 [1, 5120, 1280], P(None, 'dp', 'seq'), may hold values from -0.078125 to 0.078125
- first_contract: float32 [1, 5120, 1280], P(None, 'dp', 'seq'), may hold values from -32 to 32
- second_contract: float32 [1, 5120, 1280], P(None, 'dp', 'seq'), may hold values from 155.648 to 622.592
- gain_values: float32 [1, 2, 1280], replicated, may hold values from 0.1 to 1.9
- first_gains: float32 [1, 2, 1280], replicated, may hold values from -40 to 40
- second_gains: float32 [1, 2, 1280], replicated, may hold values from 211.3536 to 843.776
- bias_values: float32 [1, 10, 1280], replicated, may hold values from -4 to 4
- first_biases: float32 [1, 10, 1280], replicated, may hold values from -32 to 32
- second_biases: float32 [1, 10, 1280], replicated, may hold values from 108.1344 to 430.8992
Outputs:
- block_out: float32 [8, 1024, 1280], P('dp', 'seq')
- grad_tokens: float32 [8, 1024, 1280], P('dp', 'seq')
- gradient_inproj: float32 [1, 1280, 3840], P(None, 'dp', 'seq')
- momentum_inproj: float32 [1, 1280, 3840], P(None, 'dp', 'seq')
- variance_inproj: float32 [1, 1280, 3840], P(None, 'dp', 'seq')
- updated_inproj: float32 [1, 1280, 3840], P(None, 'dp', 'seq')
- gradient_outproj: float32 [1, 1280, 1280], P(None, 'dp', 'seq')
- momentum_outproj: float32 [1, 1280, 1280], P(None, 'dp', 'seq')
- variance_outproj: float32 [1, 1280, 1280], P(None, 'dp', 'seq')
- updated_outproj: float32 [1, 1280, 1280], P(None, 'dp', 'seq')
- gradient_expand: float32 [1, 1280, 5120], P(None, 'dp', 'seq')
- momentum_expand: float32 [1, 1280, 5120], P(None, 'dp', 'seq')
- variance_expand: float32 [1, 1280, 5120], P(None, 'dp', 'seq')
- updated_expand: float32 [1, 1280, 5120], P(None, 'dp', 'seq')
- gradient_contract: float32 [1, 5120, 1280], P(None, 'dp', 'seq')
- momentum_contract: float32 [1, 5120, 1280], P(None, 'dp', 'seq')
- variance_contract: float32 [1, 5120, 1280], P(None, 'dp', 'seq')
- updated_contract: float32 [1, 5120, 1280], P(None, 'dp', 'seq')
- gradient_gains: float32 [1, 2, 1280], replicated
- momentum_gains: float32 [1, 2, 1280], replicated
- variance_gains: float32 [1, 2, 1280], replicated
- updated_gains: float32 [1, 2, 1280], replicated
- gradient_biases: float32 [1, 10, 1280], replicated
- momentum_biases: float32 [1, 10, 1280], replicated
- variance_biases: float32 [1, 10, 1280], replicated
- updated_biases: float32 [1, 10, 1280], replicated
The draws below stay inside these ranges and needn't reach their ends.
All inputs are finite; a program needn't handle non-finite values.
Results may differ from the reference program's by a relative error of at most 0.01.
Values may be sent and summed in bfloat16 or wider, within the bound.
No kernel may reach another device: no remote copies, remote signals or barrier semaphores. Data moves between devices by JAX's collectives and lax.ppermute only.
A program may use at most 320 MiB of HBM per device.

```python
import math
import jax
import jax.numpy as jnp
from jax import lax

D = 1280
HEADS = 20
HEAD_DIM = 64
FF = 5120
LAYERS = 1
LEN = 1024
STEP = 10
SEQS = 8
TOKENS = 8192


def shard_levels(rng, shape, pieces, least, top_value):
    level, own = 1.0, jax.random.fold_in(rng, 6)
    for axis_at, blocks in pieces:
        steps = jnp.exp(jax.random.uniform(jax.random.fold_in(own, axis_at), (blocks,), jnp.float32, least / len(pieces), top_value / len(pieces)))
        level = level * jnp.repeat(steps, shape[axis_at] // blocks).reshape([-1 if axis == axis_at else 1 for axis in range(len(shape))])
    return level


def normal_values(rng, dims, scale, most, split=(), held_as=jnp.bfloat16):
    level = shard_levels(rng, dims, split, -0.22, 0.18) if split else 1.0
    drawn = jax.random.normal(rng, dims, jnp.float32) * scale * level
    return jnp.minimum(jnp.maximum(drawn, -most), most).astype(held_as)


def setup_inputs(seed: int = 0) -> dict:
    key_list = jax.random.split(jax.random.key(seed), 21)
    tokens = normal_values(key_list[0], (SEQS, LEN, D), 1.0, 6.0, ((0, 8), (1, 4)))
    cotangent = normal_values(key_list[1], (SEQS, LEN, D), 1.0, 6.0, ((0, 8), (1, 4)))
    weight_inproj = normal_values(key_list[2], (LAYERS, D, 3 * D), D ** -0.5, 0.15625, ((1, 8), (2, 4)), jnp.float32)
    first_inproj = normal_values(key_list[3], (LAYERS, D, 3 * D), (0.534 * (TOKENS / LEN) ** 0.5), 8.0, ((1, 8), (2, 4)), jnp.float32)
    second_inproj = jnp.clip(jnp.exp(math.log(38.48) - 1.3800767 * jax.random.uniform(key_list[4], (LAYERS, D, 3 * D), jnp.float32) ** shard_levels(key_list[4], (LAYERS, D, 3 * D), ((1, 8), (2, 4)), -0.2, 0.2)), 9.68, 38.48)
    weight_outproj = normal_values(key_list[5], (LAYERS, D, D), (D // 16) ** -0.5, 0.625, ((1, 8), (2, 4)), jnp.float32)
    first_outproj = normal_values(key_list[6], (LAYERS, D, D), (0.0333 * TOKENS ** 0.5), 16.0, ((1, 8), (2, 4)), jnp.float32)
    second_outproj = jnp.clip(jnp.exp(math.log(155.648) - 1.3968765 * jax.random.uniform(key_list[7], (LAYERS, D, D), jnp.float32) ** shard_levels(key_list[7], (LAYERS, D, D), ((1, 8), (2, 4)), -0.2, 0.2)), 38.5024, 155.648)
    weight_expand = normal_values(key_list[8], (LAYERS, D, FF), D ** -0.5, 0.15625, ((1, 8), (2, 4)), jnp.float32)
    first_expand = normal_values(key_list[9], (LAYERS, D, FF), (0.0333 * TOKENS ** 0.5), 16.0, ((1, 8), (2, 4)), jnp.float32)
    second_expand = jnp.clip(jnp.exp(math.log(155.648) - 1.3968765 * jax.random.uniform(key_list[10], (LAYERS, D, FF), jnp.float32) ** shard_levels(key_list[10], (LAYERS, D, FF), ((1, 8), (2, 4)), -0.2, 0.2)), 38.5024, 155.648)
    weight_contract = normal_values(key_list[11], (LAYERS, FF, D), FF ** -0.5, 0.078125, ((1, 8), (2, 4)), jnp.float32)
    first_contract = normal_values(key_list[12], (LAYERS, FF, D), (0.0667 * TOKENS ** 0.5), 32.0, ((1, 8), (2, 4)), jnp.float32)
    second_contract = jnp.clip(jnp.exp(math.log(622.592) - 1.3862944 * jax.random.uniform(key_list[13], (LAYERS, FF, D), jnp.float32) ** shard_levels(key_list[13], (LAYERS, FF, D), ((1, 8), (2, 4)), -0.2, 0.2)), 155.648, 622.592)
    gain_values = jnp.clip(1.0 + 0.18 * jax.random.normal(key_list[14], (LAYERS, 2, D), jnp.float32), 0.1, 1.9)
    first_gains = normal_values(key_list[15], (LAYERS, 2, D), (0.0778 * TOKENS ** 0.5), 40.0, (), jnp.float32)
    second_gains = jnp.clip(jnp.exp(jax.random.uniform(key_list[16], (LAYERS, 2, D), jnp.float32, math.log(211.3536), math.log(843.776))), 211.3536, 843.776)
    bias_values = normal_values(key_list[17], (LAYERS, 10, D), 0.3, 4.0, (), jnp.float32)
    first_biases = normal_values(key_list[18], (LAYERS, 10, D), (0.0556 * TOKENS ** 0.5), 32.0, (), jnp.float32)
    second_biases = jnp.clip(jnp.exp(jax.random.uniform(key_list[19], (LAYERS, 10, D), jnp.float32, math.log(108.1344), math.log(430.8992))), 108.1344, 430.8992)
    return dict(tokens=tokens, cotangent=cotangent, weight_inproj=weight_inproj, first_inproj=first_inproj, second_inproj=second_inproj, weight_outproj=weight_outproj, first_outproj=first_outproj, second_outproj=second_outproj, weight_expand=weight_expand, first_expand=first_expand, second_expand=second_expand, weight_contract=weight_contract, first_contract=first_contract, second_contract=second_contract, gain_values=gain_values, first_gains=first_gains, second_gains=second_gains, bias_values=bias_values, first_biases=first_biases, second_biases=second_biases)


@jax.custom_vjp
def low(v):
    return lax.optimization_barrier(v.astype(jnp.bfloat16)).astype(jnp.float32)

@jax.custom_vjp
def low_back(v):
    return v

def low_keep(v):
    return (low(v), None)

def low_pass(kept, grad):
    return (grad,)

def back_keep(v):
    return (v, None)

def back_low(kept, grad):
    return (low(grad),)
low.defvjp(low_keep, low_pass)
low_back.defvjp(back_keep, back_low)
NORM_EPS = 1e-05
BETA_ONE = 0.9
BETA_TWO = 0.95
ADAM_EPS = 1e-08
MATRIX_RATE = 0.02
VECTOR_RATE = 0.15
MATRIX_DECAY = 0.1
HIGHEST = lax.Precision.HIGHEST

def product(left, right):
    return jnp.matmul(left, right, precision=HIGHEST)

def layer_norm(values, gain, shift):
    center = values - lax.optimization_barrier(jnp.mean(values, axis=-1, keepdims=True))
    spread = lax.optimization_barrier(jnp.mean(center * center, axis=-1, keepdims=True))
    return center * lax.rsqrt(spread + NORM_EPS) * gain + shift

def attend(member):
    query, keyed, valued = member
    scores = jnp.einsum('qhd,khd->hqk', query, keyed, precision=HIGHEST) * HEAD_DIM ** (-0.5)
    scores = low_back(scores)
    rowpos = lax.broadcasted_iota(jnp.int32, scores.shape, 1)
    colpos = lax.broadcasted_iota(jnp.int32, scores.shape, 2)
    scores = jnp.where(colpos <= rowpos, scores, -1000000000.0)
    probs = low(jax.nn.softmax(scores, axis=-1))
    return jnp.einsum('hqk,khd->qhd', probs, valued, precision=HIGHEST)

def block(inputs, weights, gains, shifts):
    inproj, outproj, expand, contract = weights
    batch, length, width = inputs.shape
    normed = low(layer_norm(inputs, gains[0], shifts[0]))
    blank = jnp.zeros_like(shifts[1])
    joined = low_back(product(normed, inproj) + jnp.concatenate([shifts[1], blank, shifts[2]]))
    query = low(joined[..., :width]).reshape(batch, length, HEADS, HEAD_DIM)
    keyed = low(joined[..., width:2 * width]).reshape(batch, length, HEADS, HEAD_DIM)
    valued = low(joined[..., 2 * width:]).reshape(batch, length, HEADS, HEAD_DIM)
    attended = lax.map(jax.checkpoint(attend), (query, keyed, valued))
    attended = low(low_back(attended.reshape(batch, length, width)))
    middle = inputs + low_back(product(attended, outproj) + shifts[3])
    second = low(layer_norm(middle, gains[1], shifts[4]))
    inner = low_back(product(second, expand) + shifts[5:9].reshape(-1))
    active = low(jax.nn.gelu(inner, approximate=True))
    return middle + low_back(product(active, contract) + shifts[9])

def forward(inputs, params):
    inproj, outproj, expand, contract, gains, shifts = params
    current = inputs
    for index in range(LAYERS):
        weights = (low(inproj[index]), low(outproj[index]), low(expand[index]), low(contract[index]))
        current = block(current, weights, gains[index], shifts[index])
    return current

def adam(weight, first, second, grad, rate, decay):
    momentum = BETA_ONE * first + (1.0 - BETA_ONE) * grad
    variance = BETA_TWO * second + (1.0 - BETA_TWO) * grad * grad
    corrected = momentum / (1.0 - BETA_ONE ** STEP)
    scaled = jnp.sqrt(variance / (1.0 - BETA_TWO ** STEP))
    updated = weight - rate * (corrected / (scaled + ADAM_EPS) + decay * weight)
    return (momentum, variance, updated)

def reference(tokens, cotangent, weight_inproj, first_inproj, second_inproj, weight_outproj, first_outproj, second_outproj, weight_expand, first_expand, second_expand, weight_contract, first_contract, second_contract, gain_values, first_gains, second_gains, bias_values, first_biases, second_biases):
    params = (weight_inproj, weight_outproj, weight_expand, weight_contract, gain_values, bias_values)
    group = math.gcd(SEQS, max(1, 4096 // LEN))
    inputs = tokens.astype(jnp.float32).reshape(SEQS // group, group, LEN, D)
    cotangents = cotangent.astype(jnp.float32).reshape(SEQS // group, group, LEN, D)

    def one_group(total, member):
        group_in, group_cot = member
        output, pull = jax.vjp(forward, group_in, params)
        grad_in, grad_params = pull(group_cot)
        total = jax.tree.map(lambda left, right: left + right, total, grad_params)
        return (total, (output, grad_in))
    zeros = jax.tree.map(jnp.zeros_like, params)
    grads, (outputs, grad_inputs) = lax.scan(one_group, zeros, (inputs, cotangents))
    block_out = outputs.reshape(SEQS, LEN, D)
    grad_tokens = grad_inputs.reshape(SEQS, LEN, D)
    inproj_new = adam(weight_inproj, first_inproj, second_inproj, grads[0], MATRIX_RATE, MATRIX_DECAY)
    outproj_new = adam(weight_outproj, first_outproj, second_outproj, grads[1], MATRIX_RATE, MATRIX_DECAY)
    expand_new = adam(weight_expand, first_expand, second_expand, grads[2], MATRIX_RATE, MATRIX_DECAY)
    contract_new = adam(weight_contract, first_contract, second_contract, grads[3], MATRIX_RATE, MATRIX_DECAY)
    gains_new = adam(gain_values, first_gains, second_gains, grads[4], VECTOR_RATE, 0.0)
    biases_new = adam(bias_values, first_biases, second_biases, grads[5], VECTOR_RATE, 0.0)
    return (block_out, grad_tokens, grads[0], inproj_new[0], inproj_new[1], inproj_new[2], grads[1], outproj_new[0], outproj_new[1], outproj_new[2], grads[2], expand_new[0], expand_new[1], expand_new[2], grads[3], contract_new[0], contract_new[1], contract_new[2], grads[4], gains_new[0], gains_new[1], gains_new[2], grads[5], biases_new[0], biases_new[1], biases_new[2])
```

```python
import functools

import jax
import jax.numpy as jnp
from jax import lax
from jax.experimental import pallas as pl
from jax.experimental.pallas import tpu as pltpu
from jax.sharding import Mesh
from jax.sharding import PartitionSpec as P

HEADS = 20
HEAD_DIM = 64
STEP = 10
LANES = 128
VMEM_LIMIT = 56 * 2**20


NORM_EPS = 1e-05
BETA_ONE = 0.9
BETA_TWO = 0.95
ADAM_EPS = 1e-08
MATRIX_RATE = 0.02
VECTOR_RATE = 0.15
MATRIX_DECAY = 0.1
CONTRACT_LAST = (((1,), (1,)), ((), ()))
CONTRACT_FIRST = (((0,), (0,)), ((), ()))


def layer_norm(values, gain, shift):
    center = values - jnp.mean(values, axis=-1, keepdims=True)
    spread = jnp.mean(center * center, axis=-1, keepdims=True)
    return center * lax.rsqrt(spread + NORM_EPS) * gain + shift


def smooth_gate(values):
    return jax.nn.gelu(values, approximate=True)


def ring_of_chips(chips):
    half = chips // 2
    return list(range(half)) + list(reversed(range(half, chips)))


def chip_hop(value, direction):
    order = ring_of_chips(lax.axis_size("chip"))
    pairs = [
        (chip, order[(spot + direction) % len(order)]) for spot, chip in enumerate(order)
    ]
    return lax.ppermute(value, "chip", pairs)


def core_swap(value):
    return lax.ppermute(value, "core", [(0, 1), (1, 0)])


def seq_turn(value, distance):
    size = lax.axis_size("seq")
    return lax.ppermute(value, "seq", [(spot, (spot + distance) % size) for spot in range(size)])


def chip_at(offset):
    chips = lax.axis_size("chip")
    order = ring_of_chips(chips)
    mine = lax.axis_index("chip")
    table = [0] * chips
    for spot, chip in enumerate(order):
        table[chip] = order[(spot + offset) % chips]
    return jnp.asarray(table, jnp.int32)[mine]


def after(value, *others):
    if not others:
        return value
    return lax.optimization_barrier((value,) + others)[0]


class Queue:
    def __init__(self, depth=2):
        self.depth = depth
        self.items = []

    def gate(self, *values):
        if len(self.items) < self.depth:
            return values
        return lax.optimization_barrier(values + self.items[-self.depth])[: len(values)]

    def push(self, *values):
        self.items.append(tuple(values))

    def last(self, count=1):
        return tuple(value for item in self.items[len(self.items) - count :] for value in item)


def half_rows(rows):
    return -(-rows // 32) * 16


def row_chunks(rows, parts):
    if parts == 1:
        return [(0, rows)]
    first = rows // parts // 16 * 16
    return [(0, first), (first, rows - first)]


def send_turns(shard, distances):
    return {distance: seq_turn(shard, distance) for distance in distances}


def hold(values, *others):
    arrays = lax.optimization_barrier((*values.values(), *others))[: len(values)]
    return dict(zip(values, arrays))


def side_by_side(shard, moved):
    steps = lax.axis_size("seq")
    place = lax.axis_index("seq")
    stacked = jnp.stack([shard] + [moved[distance] for distance in range(1, steps)])
    return jnp.concatenate(
        [
            lax.dynamic_index_in_dim(stacked, lax.rem(place - spot + steps, steps), 0, False)
            for spot in range(steps)
        ],
        axis=1,
    )


class RingGather:
    def __init__(self, queue, block):
        self.queue = queue
        self.pieces = [(0, 0, block)]
        self.ahead = self.behind = block
        self.step = 0

    def advance(self, *others):
        chips = lax.axis_size("chip")
        self.ahead, self.behind = after(self.ahead, *others), after(self.behind, *others)
        self.step += 1
        step = self.step
        if step < chips // 2:
            up, down = self.queue.gate(self.ahead, self.behind)
            self.ahead, self.behind = chip_hop(up, 1), chip_hop(down, -1)
            self.pieces += [(-step, 0, self.ahead), (step, 0, self.behind)]
        else:
            half = half_rows(self.ahead.shape[0])
            up, down = self.queue.gate(self.ahead[:half], self.behind[half:])
            self.ahead, self.behind = chip_hop(up, 1), chip_hop(down, -1)
            self.pieces += [(step, 0, self.ahead), (step, half, self.behind)]
        self.queue.push(self.ahead, self.behind)


    def hold(self, *others):
        arrays = [piece for _, _, piece in self.pieces]
        arrays = lax.optimization_barrier((*arrays, *others))[: len(arrays)]
        self.pieces = [
            (offset, shift, piece)
            for (offset, shift, _), piece in zip(self.pieces, arrays)
        ]


    def hold_tail(self, count, *others):
        kept = self.pieces[:-count]
        self.pieces = self.pieces[-count:]
        self.hold(*others)
        self.pieces = kept + self.pieces


class RingReduce:
    def __init__(self, queue, block):
        self.queue = queue
        self.block = block
        self.step = lax.axis_size("chip") // 2
        self.ahead = self.behind = None
        self.halves = False

    def hold(self, *others):
        self.ahead, self.behind = after(self.ahead, *others), after(self.behind, *others)

    def arrived(self):
        ahead, behind = self.ahead.astype(jnp.float32), self.behind.astype(jnp.float32)
        if self.halves:
            return (
                jnp.concatenate([ahead, jnp.zeros_like(behind)]),
                jnp.concatenate([jnp.zeros_like(ahead), behind]),
            )
        return ahead, behind

    def advance(self, *others):
        if self.ahead is None:
            opposite = self.block(self.step)
            half = half_rows(opposite.shape[0])
            up, down = opposite[:half], opposite[half:]
            self.halves = True
        else:
            ahead, behind = self.arrived()
            up = (self.block(self.step).astype(jnp.float32) + ahead).astype(jnp.bfloat16)
            down = (self.block(-self.step).astype(jnp.float32) + behind).astype(jnp.bfloat16)
            self.halves = False
        up, down = self.queue.gate(after(up, *others), after(down, *others))
        self.ahead, self.behind = chip_hop(up, 1), chip_hop(down, -1)
        self.queue.push(self.ahead, self.behind)
        self.step -= 1

    def total(self):
        ahead, behind = self.arrived()
        return self.block(0).astype(jnp.float32) + ahead + behind


def advance_all(*rings):
    for _ in range(lax.axis_size("chip") // 2):
        for ring in rings:
            ring.advance()


def whole_vmem():
    return pl.BlockSpec(memory_space=pltpu.VMEM)


def whole_any():
    return pl.BlockSpec(memory_space=pl.ANY)


def place_kernel(plan, starts, *refs):
    sources, target, sems = refs[:-2], refs[-2], refs[-1]
    copies = []
    for spot, (which, first, rows) in enumerate(plan):
        source = sources[which].at[pl.ds(first, rows), :]
        place = pl.multiple_of(starts[spot], 16)
        copies.append(
            pltpu.make_async_copy(source, target.at[pl.ds(place, rows), :], sems.at[spot])
        )
    for copy in copies:
        copy.start()
    for copy in copies:
        copy.wait()


def put_together(rows, arrays, moves):
    starts = jnp.stack([jnp.asarray(move[3], jnp.int32) for move in moves])
    plan = [move[:3] for move in moves]
    cols = arrays[0].shape[1]
    moved = 2 * rows * cols
    return pl.pallas_call(
        functools.partial(place_kernel, plan),
        out_shape=jax.ShapeDtypeStruct((rows, cols), arrays[0].dtype),
        in_specs=[pl.BlockSpec(memory_space=pltpu.SMEM)] + [whole_any()] * len(arrays),
        out_specs=whole_vmem(),
        scratch_shapes=[pltpu.SemaphoreType.DMA((len(moves),))],
        compiler_params=pltpu.CompilerParams(vmem_limit_bytes=VMEM_LIMIT),
        cost_estimate=pl.CostEstimate(flops=0, bytes_accessed=2 * moved, transcendentals=0),
    )(starts, *arrays)


def rows_of_core(gather, rows):
    arrays = [piece for _, _, piece in gather.pieces]
    moves = [
        (spot, 0, piece.shape[0], chip_at(offset) * rows + shift)
        for spot, (offset, shift, piece) in enumerate(gather.pieces)
    ]
    return put_together(lax.axis_size("chip") * rows, arrays, moves)


def rows_of_both(gather, rows, groups):
    core = lax.axis_index("core")
    arrays, moves = [], []
    taken = 0
    for size in groups:
        pieces = gather.pieces[taken : taken + size]
        taken += size
        block = jnp.concatenate([piece for _, _, piece in pieces])
        if arrays:
            block = after(block, arrays[-1])
        arrays += [block, core_swap(block)]
        first = 0
        for offset, shift, piece in pieces:
            count = piece.shape[0]
            chip = chip_at(offset)
            moves.append((len(arrays) - 2, first, count, (2 * chip + core) * rows + shift))
            moves.append((len(arrays) - 1, first, count, (2 * chip + 1 - core) * rows + shift))
            first += count
    return put_together(lax.axis_size("chip") * 2 * rows, arrays, moves)


def mix_cores(packed, chips, low_rows, steps):
    core = lax.axis_index("core")
    both = packed.reshape(chips * low_rows, steps, 2, -1)
    halves = [
        jnp.concatenate([both[:, spot, which] for spot in range(steps)], axis=1)
        .reshape(chips, 1, low_rows, -1)
        for which in range(2)
    ]
    mine = jnp.concatenate(halves, axis=1).reshape(chips, 1, 2 * low_rows, -1)
    theirs = core_swap(mine)
    first = jnp.where(core == 0, mine, theirs)
    second = jnp.where(core == 0, theirs, mine)
    return jnp.concatenate([first, second], axis=1).reshape(chips * 4 * low_rows, -1)


def split_parts(total):
    steps = lax.axis_size("seq")
    place = lax.axis_index("seq")
    cols = total.shape[1] // steps
    low = total.astype(jnp.bfloat16)
    parts = jnp.stack([low[:, spot * cols : (spot + 1) * cols] for spot in range(steps)])
    return [
        lax.dynamic_index_in_dim(parts, lax.rem(place + distance, steps), 0, False)
        for distance in range(steps)
    ]


def send_parts(parts, distances, moved):
    for distance in distances:
        moved[distance] = seq_turn(parts[distance], distance)


def part_sum(parts, moved):
    answer = parts[0].astype(jnp.float32)
    for part in moved.values():
        answer = answer + part.astype(jnp.float32)
    return answer


def product_rows(left, right):
    whole = lax.dot_general(left, right, CONTRACT_FIRST, preferred_element_type=jnp.float32)
    return whole.astype(jnp.bfloat16)


def sum_over_seq(total):
    steps = lax.axis_size("seq")
    cols = total.shape[1] // steps
    parts = jnp.stack([total[:, spot * cols : (spot + 1) * cols] for spot in range(steps)])
    return lax.psum_scatter(parts, "seq", scatter_dimension=0, tiled=False)


def start_reduce(queue, whole, rows, parts):
    def chunk(first, count):
        def block(offset):
            return lax.dynamic_slice_in_dim(whole, chip_at(offset) * rows + first, count, 0)

        return RingReduce(queue, block)

    return [chunk(first, count) for first, count in row_chunks(rows, parts)]


def own_core_columns(values, core):
    chips = lax.axis_size("chip")
    rows = values.shape[1] // (2 * chips)
    halves = []
    for which in range(2):
        halves.append(
            jnp.concatenate(
                [values[:, (2 * chip + which) * rows : (2 * chip + which + 1) * rows] for chip in range(chips)],
                axis=1,
            )
        )
    return jnp.where(core == 0, halves[0], halves[1])


def both_tokens(values):
    return jnp.concatenate([values, core_swap(values)])


def both_left(values):
    core = lax.axis_index("core")
    mine = own_core_columns(values, core)
    theirs = own_core_columns(values, 1 - core)
    return jnp.concatenate([mine, core_swap(theirs)])


def total_along(value, axes):
    for axis in axes:
        size = lax.axis_size(axis)
        reach = 1
        while reach < size:
            value = value + lax.ppermute(value, axis, [(spot, spot ^ reach) for spot in range(size)])
            reach *= 2
    return value


def lanes_up(count):
    return -(-count // LANES) * LANES


def split_kernel(steps, parts, each, source, target):
    wide = parts * each
    for spot in range(steps):
        for part in range(parts):
            first = part * HEADS * HEAD_DIM + spot * each
            count = max(0, min(each, HEADS * HEAD_DIM - spot * each))
            if count:
                target[spot, :, part * each : part * each + count] = source[:, first : first + count]
            if count < each:
                target[spot, :, part * each + count : (part + 1) * each] = jnp.zeros(
                    (target.shape[1], each - count), target.dtype
                )
        if wide < target.shape[2]:
            target[spot, :, wide:] = jnp.zeros(
                (target.shape[1], target.shape[2] - wide), target.dtype
            )


def join_kernel(steps, parts, each, source, target):
    for spot in range(steps):
        count = max(0, min(each, HEADS * HEAD_DIM - spot * each))
        for part in range(parts):
            if count:
                first = part * HEADS * HEAD_DIM + spot * each
                target[:, first : first + count] = source[spot, :, part * each : part * each + count]


def move_kernel(kernel, shape, value):
    return pl.pallas_call(
        kernel,
        out_shape=jax.ShapeDtypeStruct(shape, value.dtype),
        in_specs=[whole_vmem()],
        out_specs=whole_vmem(),
        compiler_params=pltpu.CompilerParams(vmem_limit_bytes=VMEM_LIMIT),
        cost_estimate=pl.CostEstimate(
            flops=0, bytes_accessed=4 * value.size, transcendentals=0
        ),
    )(value)


def to_heads(values, parts):
    steps = lax.axis_size("seq")
    each = -(-HEADS // steps) * HEAD_DIM
    tokens = values.shape[0]
    shape = (steps, tokens, lanes_up(parts * each))
    split = move_kernel(functools.partial(split_kernel, steps, parts, each), shape, values)
    return lax.all_to_all(split, "seq", 0, 0)


def from_heads(values, parts):
    steps, tokens, _ = values.shape
    each = -(-HEADS // steps) * HEAD_DIM
    blocks = lax.all_to_all(values, "seq", 0, 0)
    shape = (tokens, parts * HEADS * HEAD_DIM)
    return move_kernel(functools.partial(join_kernel, steps, parts, each), shape, blocks)


def causal_scores(query, keyed, first):
    scores = lax.dot_general(query, keyed, CONTRACT_LAST, preferred_element_type=jnp.float32)
    scores = scores * HEAD_DIM ** (-0.5)
    rowpos = first + lax.broadcasted_iota(jnp.int32, scores.shape, 0)
    colpos = lax.broadcasted_iota(jnp.int32, scores.shape, 1)
    return jnp.where(colpos <= rowpos, scores, -1000000000.0)


def attend_kernel(heads, held, out_ref, log_ref):
    steps, local = held.shape[:2]
    width = heads * HEAD_DIM
    if width < out_ref.shape[2]:
        out_ref[:, :, width:] = jnp.zeros(
            (steps, local, out_ref.shape[2] - width), out_ref.dtype
        )
    for head in range(heads):
        lanes = slice(head * HEAD_DIM, (head + 1) * HEAD_DIM)
        keyed = held[:, :, width + head * HEAD_DIM : width + (head + 1) * HEAD_DIM]
        valued = held[:, :, 2 * width + head * HEAD_DIM : 2 * width + (head + 1) * HEAD_DIM]
        keyed = keyed.reshape(steps * local, HEAD_DIM)
        valued = valued.reshape(steps * local, HEAD_DIM)
        for block in range(steps):
            reach = (block + 1) * local
            query = held[block, :, lanes]
            scores = causal_scores(query, keyed[:reach], block * local)
            topmost = jnp.max(scores, axis=-1, keepdims=True)
            powers = jnp.exp(scores - topmost)
            totals = jnp.sum(powers, axis=-1, keepdims=True)
            probs = (powers * (1.0 / totals)).astype(jnp.bfloat16)
            output = jnp.dot(probs, valued[:reach], preferred_element_type=jnp.float32)
            log_ref[block, :, head : head + 1] = topmost + jnp.log(totals)
            out_ref[block, :, lanes] = output.astype(jnp.bfloat16)


def attend_back_kernel(heads, held, pulled, log_ref, out_ref, key_sum, value_sum):
    steps, local = held.shape[:2]
    width = heads * HEAD_DIM
    if 3 * width < out_ref.shape[2]:
        out_ref[:, :, 3 * width :] = jnp.zeros(
            (steps, local, out_ref.shape[2] - 3 * width), out_ref.dtype
        )
    scale = HEAD_DIM ** (-0.5)
    for head in range(heads):
        lanes = slice(head * HEAD_DIM, (head + 1) * HEAD_DIM)
        key_lanes = slice(width + head * HEAD_DIM, width + (head + 1) * HEAD_DIM)
        value_lanes = slice(2 * width + head * HEAD_DIM, 2 * width + (head + 1) * HEAD_DIM)
        keyed = held[:, :, key_lanes].reshape(steps * local, HEAD_DIM)
        valued = held[:, :, value_lanes].reshape(steps * local, HEAD_DIM)
        for block in reversed(range(steps)):
            reach = (block + 1) * local
            query = held[block, :, lanes]
            pull = pulled[block, :, lanes]
            scores = causal_scores(query, keyed[:reach], block * local)
            probs = jnp.exp(scores - log_ref[block, :, head : head + 1])
            grad_probs = lax.dot_general(
                pull, valued[:reach], CONTRACT_LAST, preferred_element_type=jnp.float32
            )
            inner = jnp.sum(grad_probs * probs, axis=-1, keepdims=True)
            grad_scores = (probs * (grad_probs - inner)).astype(jnp.bfloat16)
            grad_query = jnp.dot(grad_scores, keyed[:reach], preferred_element_type=jnp.float32)
            grad_key = lax.dot_general(
                grad_scores, query, CONTRACT_FIRST, preferred_element_type=jnp.float32
            )
            grad_value = lax.dot_general(
                probs.astype(jnp.bfloat16), pull, CONTRACT_FIRST, preferred_element_type=jnp.float32
            )
            if block == steps - 1:
                key_sum[...] = grad_key
                value_sum[...] = grad_value
            else:
                key_sum[:reach, :] += grad_key
                value_sum[:reach, :] += grad_value
            out_ref[block, :, lanes] = (grad_query * scale).astype(jnp.bfloat16)
        for block in range(steps):
            rows = slice(block * local, (block + 1) * local)
            out_ref[block, :, key_lanes] = (key_sum[rows, :] * scale).astype(jnp.bfloat16)
            out_ref[block, :, value_lanes] = value_sum[rows, :].astype(jnp.bfloat16)


def attend_forward(held):
    steps, local, _ = held.shape
    heads = -(-HEADS // steps)
    width = lanes_up(heads * HEAD_DIM)
    return pl.pallas_call(
        functools.partial(attend_kernel, heads),
        out_shape=(
            jax.ShapeDtypeStruct((steps, local, width), jnp.bfloat16),
            jax.ShapeDtypeStruct((steps, local, LANES), jnp.float32),
        ),
        in_specs=[whole_vmem()],
        out_specs=(whole_vmem(), whole_vmem()),
        compiler_params=pltpu.CompilerParams(vmem_limit_bytes=VMEM_LIMIT),
        cost_estimate=pl.CostEstimate(flops=10**9, bytes_accessed=4 * 10**6, transcendentals=10**6),
    )(held)


def attend_backward(held, pulled, logsum):
    steps, local, triple = held.shape
    heads = -(-HEADS // steps)
    return pl.pallas_call(
        functools.partial(attend_back_kernel, heads),
        out_shape=jax.ShapeDtypeStruct((steps, local, triple), jnp.bfloat16),
        in_specs=[whole_vmem()] * 3,
        out_specs=whole_vmem(),
        scratch_shapes=[
            pltpu.VMEM((steps * local, HEAD_DIM), jnp.float32),
            pltpu.VMEM((steps * local, HEAD_DIM), jnp.float32),
        ],
        compiler_params=pltpu.CompilerParams(vmem_limit_bytes=VMEM_LIMIT),
        cost_estimate=pl.CostEstimate(flops=10**9, bytes_accessed=4 * 10**6, transcendentals=10**6),
    )(held, pulled, logsum)


def layer(tokens, cotangent, shards, gains, shifts):
    chips = lax.axis_size("chip")
    core = lax.axis_index("core")
    steps = lax.axis_size("seq")
    place = lax.axis_index("seq")
    seqs, local, width = tokens.shape
    count = seqs * local
    turns = chips // 2

    inproj, outproj, expand, contract = [shard.astype(jnp.bfloat16) for shard in shards]
    rows, long_rows = inproj.shape[0], contract.shape[0]
    half = expand.shape[1] // 2
    kept = lax.dynamic_slice_in_dim(expand, core * half, half, 1)
    given = core_swap(lax.dynamic_slice_in_dim(expand, (1 - core) * half, half, 1))
    expand = jnp.concatenate(
        [jnp.where(core == 0, kept, given), jnp.where(core == 0, given, kept)]
    )

    rows_in = tokens.astype(jnp.float32).reshape(count, width)
    grad_low = cotangent.reshape(count, width)
    grad = grad_low.astype(jnp.float32)
    normed = layer_norm(rows_in, gains[0], shifts[0]).astype(jnp.bfloat16)

    inproj_moved = send_turns(inproj, range(1, steps))
    inproj_ring = RingGather(Queue(), side_by_side(inproj, inproj_moved))
    inproj_ring.advance(given)
    inproj_first = inproj_ring.queue.last()
    expand = lax.all_gather(after(expand, *inproj_moved.values()), "seq", axis=1, tiled=True)
    contract = lax.all_gather(after(contract, *inproj_moved.values()), "seq", axis=1, tiled=True)
    for _ in range(turns - 1):
        inproj_ring.advance()
    inproj_last = inproj_ring.queue.last()
    expand = lax.all_gather(after(expand, *inproj_last), "chip", axis=0, tiled=True)
    outproj_moved = send_turns(after(outproj, *inproj_moved.values()), range(1, steps))
    pieces = len(inproj_ring.pieces)
    inproj = rows_of_both(inproj_ring, rows, [pieces - 2, 2])

    blank = jnp.zeros_like(shifts[1])
    joined = jnp.dot(normed, inproj, preferred_element_type=jnp.float32) + jnp.concatenate(
        [shifts[1], blank, shifts[2]]
    )
    joined = joined.astype(jnp.bfloat16)
    held = to_heads(joined, 3)
    contract = lax.all_gather(after(contract, joined), "chip", axis=0, tiled=True)
    outproj_ring = RingGather(Queue(), side_by_side(outproj, hold(outproj_moved, joined)))
    outproj_ring.advance()
    outproj_first = outproj_ring.queue.last()
    for _ in range(turns - 1):
        outproj_ring.advance()
    outproj = rows_of_both(outproj_ring, rows, [pieces])
    held = after(held, outproj)
    attended, logsum = attend_forward(held)
    attended = from_heads(attended, 1)
    middle = rows_in + (jnp.dot(attended, outproj, preferred_element_type=jnp.float32) + shifts[3])
    second = layer_norm(middle, gains[1], shifts[4]).astype(jnp.bfloat16)

    second_both = both_tokens(second)
    grad_both = both_tokens(grad_low)
    hidden = shifts[5:9].reshape(steps, 2, -1)
    hidden = lax.dynamic_index_in_dim(hidden, core, 1, False).reshape(-1)
    inner = jnp.dot(second_both, expand, preferred_element_type=jnp.float32) + hidden
    active = smooth_gate(inner).astype(jnp.bfloat16)
    contract_whole = product_rows(active, grad_both)
    contract_total = lax.psum_scatter(contract_whole, "chip", scatter_dimension=0, tiled=True)

    bias_contract = jnp.sum(grad_low, axis=0, dtype=jnp.float32)
    grad_active = lax.dot_general(
        after(grad_both, contract_whole), contract, CONTRACT_LAST, preferred_element_type=jnp.float32
    )
    gate_pull = jax.vjp(smooth_gate, inner)[1]
    grad_inner = gate_pull(grad_active)[0].astype(jnp.bfloat16)
    grad_second = lax.dot_general(
        grad_inner, expand, CONTRACT_LAST, preferred_element_type=jnp.float32
    )
    expand_whole = product_rows(after(second_both, grad_second), grad_inner)
    expand_total = lax.psum_scatter(expand_whole, "chip", scatter_dimension=0, tiled=True)
    bias_expand = jnp.sum(grad_inner, axis=0, dtype=jnp.float32).reshape(steps, 1, -1)
    bias_expand = jnp.where(
        jnp.arange(2)[None, :, None] == core, bias_expand, 0.0
    ).reshape(4, width)
    grad_second = grad_second[:count] + core_swap(grad_second[count:])
    grad_second = after(grad_second, expand_whole)
    norm_pull = jax.vjp(layer_norm, middle, gains[1], shifts[4])[1]
    grad_middle_norm, gain_two, shift_two = norm_pull(grad_second)
    grad_middle = grad + grad_middle_norm
    branch_low = grad_middle.astype(jnp.bfloat16)
    bias_outproj = jnp.sum(branch_low, axis=0, dtype=jnp.float32)
    grad_attended = lax.dot_general(
        branch_low, outproj, CONTRACT_LAST, preferred_element_type=jnp.float32
    ).astype(jnp.bfloat16)
    pulled = to_heads(grad_attended, 1)

    partial = jnp.dot(after(active, grad_attended), contract, preferred_element_type=jnp.float32)
    output = middle + (partial[:count] + core_swap(partial[count:]) + shifts[9])
    outproj_whole = product_rows(both_left(attended), both_tokens(after(branch_low, grad_attended)))
    outproj_queue = Queue(1)
    (outproj_sum,) = start_reduce(outproj_queue, outproj_whole, rows, 1)
    outproj_sum.advance()
    pulled = after(pulled, output, contract_total, *outproj_queue.last())
    grad_heads = attend_backward(held, pulled, logsum)
    outproj_sum.hold(grad_heads)
    for _ in range(turns - 1):
        outproj_sum.advance()
    outproj_last = outproj_queue.last()
    contract_grad = sum_over_seq(after(contract_total, grad_heads))
    outproj_parts = split_parts(outproj_sum.total())
    normed_both = both_left(after(normed, grad_heads))
    grad_joined = after(
        from_heads(grad_heads, 3), expand_total, normed_both, *outproj_parts[1:]
    )
    expand_own = sum_over_seq(after(expand_total, grad_joined))

    joined_both = both_tokens(grad_joined)
    inproj_whole = product_rows(normed_both, joined_both)
    inproj_sums = start_reduce(Queue(2), inproj_whole, rows, 2)
    advance_all(*inproj_sums)
    inproj_items = inproj_sums[0].queue.items
    outproj_moved = {}
    send_parts([after(part, grad_joined) for part in outproj_parts], range(1, steps), outproj_moved)
    inproj_grad = []
    inproj_moved = []
    for part in inproj_sums:
        parts, moved = split_parts(part.total()), {}
        send_parts(parts, range(1, steps), moved)
        inproj_moved += list(moved.values())
        inproj_grad.append(part_sum(parts, moved))
    inproj_grad = jnp.concatenate(inproj_grad)
    outproj_grad = part_sum(outproj_parts, hold(outproj_moved, *inproj_moved[: steps - 1]))
    contract_grad = after(contract_grad, *inproj_moved[: steps - 1]).astype(jnp.float32)
    expand_own = after(expand_own, *inproj_moved[: steps - 1]).astype(jnp.float32)
    kept = lax.dynamic_slice_in_dim(expand_own, core * rows, rows, 0)
    given = core_swap(lax.dynamic_slice_in_dim(expand_own, (1 - core) * rows, rows, 0))
    expand_grad = jnp.concatenate(
        [jnp.where(core == 0, kept, given), jnp.where(core == 0, given, kept)], axis=1
    )

    bias_query = jnp.sum(grad_joined[:, :width], axis=0, dtype=jnp.float32)
    bias_value = jnp.sum(grad_joined[:, 2 * width :], axis=0, dtype=jnp.float32)
    grad_normed = lax.dot_general(
        grad_joined, inproj, CONTRACT_LAST, preferred_element_type=jnp.float32
    )
    first_pull = jax.vjp(layer_norm, rows_in, gains[0], shifts[0])[1]
    grad_rows, gain_one, shift_one = first_pull(grad_normed)
    grad_out = grad_middle + grad_rows
    sums = total_along(
        jnp.concatenate(
            [
                jnp.stack(
                    [gain_one, gain_two, shift_one, bias_query, bias_value, bias_outproj, shift_two]
                ),
                bias_expand,
                bias_contract[None],
            ]
        ),
        ("core", "chip"),
    )
    sums = total_along(after(sums, *inproj_items[0]), ("seq",))
    return (
        output.reshape(tokens.shape),
        grad_out.reshape(tokens.shape),
        (inproj_grad, outproj_grad, expand_grad, contract_grad),
        sums[:2],
        sums[2:],
    )


def adam(weight, first, second, grad, rate, decay):
    momentum = BETA_ONE * first + (1.0 - BETA_ONE) * grad
    variance = BETA_TWO * second + (1.0 - BETA_TWO) * grad * grad
    corrected = momentum / (1.0 - BETA_ONE**STEP)
    scaled = jnp.sqrt(variance / (1.0 - BETA_TWO**STEP))
    updated = weight - rate * (corrected / (scaled + ADAM_EPS) + decay * weight)
    return (momentum, variance, updated)


def body(
    tokens,
    cotangent,
    weight_inproj,
    first_inproj,
    second_inproj,
    weight_outproj,
    first_outproj,
    second_outproj,
    weight_expand,
    first_expand,
    second_expand,
    weight_contract,
    first_contract,
    second_contract,
    gain_values,
    first_gains,
    second_gains,
    bias_values,
    first_biases,
    second_biases,
):
    current, grad, matrices, gain_total, shift_total = layer(
        tokens,
        cotangent,
        (weight_inproj[0], weight_outproj[0], weight_expand[0], weight_contract[0]),
        gain_values[0],
        bias_values[0],
    )
    inproj_grad, outproj_grad, expand_grad, contract_grad = [member[None] for member in matrices]
    gain_total, shift_total = (gain_total[None], shift_total[None])
    inproj_new = adam(
        weight_inproj, first_inproj, second_inproj, inproj_grad, MATRIX_RATE, MATRIX_DECAY
    )
    outproj_new = adam(
        weight_outproj, first_outproj, second_outproj, outproj_grad, MATRIX_RATE, MATRIX_DECAY
    )
    expand_new = adam(
        weight_expand, first_expand, second_expand, expand_grad, MATRIX_RATE, MATRIX_DECAY
    )
    contract_new = adam(
        weight_contract, first_contract, second_contract, contract_grad, MATRIX_RATE, MATRIX_DECAY
    )
    gains_new = adam(gain_values, first_gains, second_gains, gain_total, VECTOR_RATE, 0.0)
    biases_new = adam(bias_values, first_biases, second_biases, shift_total, VECTOR_RATE, 0.0)
    return (
        current,
        grad,
        inproj_grad,
        inproj_new[0],
        inproj_new[1],
        inproj_new[2],
        outproj_grad,
        outproj_new[0],
        outproj_new[1],
        outproj_new[2],
        expand_grad,
        expand_new[0],
        expand_new[1],
        expand_new[2],
        contract_grad,
        contract_new[0],
        contract_new[1],
        contract_new[2],
        gain_total,
        gains_new[0],
        gains_new[1],
        gains_new[2],
        shift_total,
        biases_new[0],
        biases_new[1],
        biases_new[2],
    )


def solution(mesh):
    size, steps = mesh.devices.shape
    mesh = Mesh(mesh.devices.reshape(size // 2, 2, steps), ("chip", "core", "seq"))
    return jax.shard_map(
        body,
        mesh=mesh,
        in_specs=(
            P(("chip", "core"), "seq", None),
            P(("chip", "core"), "seq", None),
            P(None, ("chip", "core"), "seq"),
            P(None, ("chip", "core"), "seq"),
            P(None, ("chip", "core"), "seq"),
            P(None, ("chip", "core"), "seq"),
            P(None, ("chip", "core"), "seq"),
            P(None, ("chip", "core"), "seq"),
            P(None, ("chip", "core"), "seq"),
            P(None, ("chip", "core"), "seq"),
            P(None, ("chip", "core"), "seq"),
            P(None, ("chip", "core"), "seq"),
            P(None, ("chip", "core"), "seq"),
            P(None, ("chip", "core"), "seq"),
            P(),
            P(),
            P(),
            P(),
            P(),
            P(),
        ),
        out_specs=(
            P(("chip", "core"), "seq", None),
            P(("chip", "core"), "seq", None),
            P(None, ("chip", "core"), "seq"),
            P(None, ("chip", "core"), "seq"),
            P(None, ("chip", "core"), "seq"),
            P(None, ("chip", "core"), "seq"),
            P(None, ("chip", "core"), "seq"),
            P(None, ("chip", "core"), "seq"),
            P(None, ("chip", "core"), "seq"),
            P(None, ("chip", "core"), "seq"),
            P(None, ("chip", "core"), "seq"),
            P(None, ("chip", "core"), "seq"),
            P(None, ("chip", "core"), "seq"),
            P(None, ("chip", "core"), "seq"),
            P(None, ("chip", "core"), "seq"),
            P(None, ("chip", "core"), "seq"),
            P(None, ("chip", "core"), "seq"),
            P(None, ("chip", "core"), "seq"),
            P(),
            P(),
            P(),
            P(),
            P(),
            P(),
            P(),
            P(),
        ),
        check_vma=False,
    )
```
